256 devices in a mesh: replica: 16 (over z_lo, y), fsdp: 16 (over z_hi, x, core).
Axes of the slice: x: 4, y: 4, z: 8 (z_hi: 2, z_lo: 4; z = z_hi * 4 + z_lo), core: 2. Of those that a mesh axis runs over, the one named last changes fastest.
Arguments:
- tokens: bfloat16 [65536, 8192], P(('replica', 'fsdp')), may hold values from -24 to 24
- cotangent: bfloat16 [65536, 512], P(('replica', 'fsdp')), may hold values from -6 to 6
- w_value: bfloat16 [16, 8192, 512], P('replica', 'fsdp'), may hold values from -0.0625 to 0.0625
- outer_global: float32 [8, 256, 1024], P(None, 'fsdp'), may hold values from -6 to 6
- outer_momentum: float32 [8, 256, 1024], P(None, 'fsdp'), may hold values from -6 to 6
- local_params: float32 [16, 8, 256, 1024], P('replica', None, 'fsdp'), may hold values from -6 to 6
- outer_delta: float32 [16, 256, 1024], P('replica', 'fsdp'), may hold values from -6 to 6
- fragment: int32 [1], replicated, may hold values from 0 to 7
Outputs:
- values: bfloat16 [65536, 512], P(('replica', 'fsdp'))
- grad_tokens: bfloat16 [65536, 8192], P(('replica', 'fsdp'))
- grad_weight: float32 [16, 8192, 512], P('replica', 'fsdp')
- new_global: float32 [256, 1024], P('fsdp')
- new_momentum: float32 [256, 1024], P('fsdp')
- new_local: float32 [16, 256, 1024], P('replica', 'fsdp')
The draws below stay inside these ranges and needn't reach their ends.
All inputs are finite; a program needn't handle non-finite values.
Results may differ from the reference program's by a relative error of at most 0.01.
Values may be sent and summed in bfloat16 or wider, within the bound.
No kernel may reach another device: no remote copies, remote signals or barrier semaphores. Data moves between devices by JAX's collectives and lax.ppermute only.
A program may use at most 128 MiB of HBM per device.

```python
import jax
import jax.numpy as jnp
from jax import lax

D = 8192
VW = 512
TOK_DEV = 256
TOKENS = 65536
NFRAG = 8
FW = 1024
FROWS = 256
N_REPLICA = 16
N_FSDP = 16


def with_spikes(array, own_key, source, target, blocks, factor):
    def block_of(axis_at):
        return (jnp.arange(array.shape[axis_at]) // (array.shape[axis_at] // blocks)).reshape((-1,) + (1,) * (array.ndim - 1 - axis_at))

    one_side = jax.random.permutation(own_key, blocks)[block_of(target)]
    other_side = (block_of(target) + blocks // 2) % blocks
    return jnp.where((block_of(source) == one_side) | (block_of(source) == other_side), factor * array, array)


def block_levels(key, extent, cuts, smallest, high):
    gain = 1.0
    for dim, blocks in cuts:
        heights = jax.random.uniform(jax.random.fold_in(jax.random.fold_in(key, 6), dim), (blocks,), jnp.float32, smallest / len(cuts), high / len(cuts))
        gain = gain * jnp.repeat(jnp.exp(heights), extent[dim] // blocks).reshape((-1,) + (1,) * (len(extent) - 1 - dim))
    return gain


def gaussian(key, shape, width, bound, split=(), dtype=jnp.bfloat16):
    entries = width * jax.random.normal(key, shape, jnp.float32)
    if split:
        entries = entries * block_levels(key, shape, split, -0.22, 0.18)
    return jnp.clip(entries, -bound, bound).astype(dtype)


def heavy_noise(rng, dims, spread, bound, pieces, heavy, dtype=jnp.bfloat16):
    values = spread * jax.random.normal(rng, dims, jnp.float32)
    if pieces:
        values = values * block_levels(rng, dims, pieces, -0.22, 0.18)
    return jnp.clip(with_spikes(values, jax.random.fold_in(rng, 3), *heavy), -bound, bound).astype(dtype)


def setup_inputs(seed: int = 0) -> dict:
    key_of = jax.random.split(jax.random.key(seed), 9)
    return {
        "tokens": heavy_noise(key_of[0], (TOKENS, D), 1.0, 24.0, ((0, 256),), (0, 1, 256, 6.0)),
        "cotangent": gaussian(key_of[1], (TOKENS, VW), 1.0, 6.0, ((0, 256),)),
        "w_value": gaussian(key_of[2], (N_REPLICA, D, VW), D ** -0.5, 0.0625, ((0, 16), (1, 16))),
        "outer_global": gaussian(key_of[3], (NFRAG, FROWS, FW), 1.0, 6.0, ((1, 16),), jnp.float32),
        "outer_momentum": gaussian(key_of[4], (NFRAG, FROWS, FW), 0.5, 6.0, ((1, 16),), jnp.float32),
        "local_params": gaussian(key_of[5], (N_REPLICA, NFRAG, FROWS, FW), 1.0, 6.0, ((0, 16), (2, 16)), jnp.float32),
        "outer_delta": gaussian(key_of[6], (N_REPLICA, FROWS, FW), 1.0, 6.0, ((0, 16), (1, 16)), jnp.float32),
        "fragment": jax.random.randint(key_of[7], (1,), 0, NFRAG).astype(jnp.int32),
    }


outer_rate = 0.7
momentum_decay = 0.9
mix_weight = 0.5


def reference(tokens, cotangent, w_value, outer_global, outer_momentum, local_params, outer_delta, fragment):
    group_rows = TOK_DEV * N_FSDP
    grouped_tokens = tokens.reshape(N_REPLICA, group_rows, D)
    grouped_cotangent = cotangent.reshape(N_REPLICA, group_rows, VW)

    def replica_step(item):
        inputs, upstream, weight = item
        projected = jnp.dot(inputs, weight, preferred_element_type=jnp.float32).astype(jnp.bfloat16)
        back = lax.dot_general(upstream, weight, (((1,), (1,)), ((), ())), preferred_element_type=jnp.float32).astype(jnp.bfloat16)
        weight_grad = lax.dot_general(inputs, upstream, (((0,), (0,)), ((), ())), preferred_element_type=jnp.float32)
        return projected, back, weight_grad

    values, grad_tokens, grad_weight = lax.map(replica_step, (grouped_tokens, grouped_cotangent, w_value))
    values = values.reshape(TOKENS, VW)
    grad_tokens = grad_tokens.reshape(TOKENS, D)
    fragment_id = fragment[0]
    chosen_global = lax.dynamic_index_in_dim(outer_global, fragment_id, 0, keepdims=False)
    chosen_moment = lax.dynamic_index_in_dim(outer_momentum, fragment_id, 0, keepdims=False)
    chosen_local = lax.dynamic_index_in_dim(local_params, fragment_id, 1, keepdims=False)
    averaged = jnp.sum(outer_delta, axis=0) / N_REPLICA
    new_momentum = momentum_decay * chosen_moment + averaged
    new_global = chosen_global - outer_rate * (averaged + momentum_decay * new_momentum)
    new_local = mix_weight * chosen_local + (1.0 - mix_weight) * new_global[None]
    return values, grad_tokens, grad_weight, new_global, new_momentum, new_local
```

```python
import jax
import jax.numpy as jnp
from jax import lax
from jax.experimental import pallas as pl
from jax.experimental.pallas import tpu as pltpu
from jax.sharding import PartitionSpec as P

outer_rate = 0.7
momentum_decay = 0.9
mix_weight = 0.5

f32, bf16 = jnp.float32, jnp.bfloat16
VMEM_LIMIT = 32 * 1024 * 1024
NX, NZ, NC = 4, 2, 2


def fsdp_perm(dz, dx, dc):
    pairs = []
    for z in range(NZ):
        for x in range(NX):
            for c in range(NC):
                there = (((z + dz) % NZ) * NX + (x + dx) % NX) * NC + (c + dc) % NC
                pairs.append(((z * NX + x) * NC + c, there))
    return pairs


PLUS, MINUS = fsdp_perm(0, 1, 0), fsdp_perm(0, -1, 0)
ACROSS, OTHER_CORE = fsdp_perm(1, 0, 0), fsdp_perm(0, 0, 1)


def send(array, pairs):
    return lax.ppermute(array, "fsdp", pairs)


def params(**more):
    return pltpu.CompilerParams(vmem_limit_bytes=VMEM_LIMIT, **more)


def dot(a, b, ca, cb):
    return lax.dot_general(a, b, (((ca,), (cb,)), ((), ())), preferred_element_type=f32)


def select_kernel(places, tokens, cotangent, out):
    step = pl.program_id(0)

    @pl.when(step < 8)
    def _():
        out[0] = tokens[...]

    @pl.when(step == 8)
    def _():
        out[0] = cotangent[...]


def select(places, tokens, cotangent):
    rows, width = cotangent.shape
    return pl.pallas_call(
        select_kernel,
        grid_spec=pltpu.PrefetchScalarGridSpec(
            num_scalar_prefetch=1,
            grid=(9,),
            in_specs=[
                pl.BlockSpec((rows, width), lambda i, p: (0, p[i])),
                pl.BlockSpec((rows, width), lambda i, p: (0, 0)),
            ],
            out_specs=pl.BlockSpec((1, rows, width), lambda i, p: (i, 0, 0)),
        ),
        out_shape=jax.ShapeDtypeStruct((9, rows, width), bf16),
        compiler_params=params(),
        cost_estimate=pl.CostEstimate(flops=0, bytes_accessed=18 * rows * width * 2, transcendentals=0),
        name="select",
    )(places, tokens, cotangent)


def far_kernel(places, tokens, cot, par, par_cot, top, bottom):
    block = dot(tokens[...], cot[...], 0, 0) + dot(par[0], par_cot[0], 0, 0)
    half = block.shape[0] // 2
    top[0] = block[:half].astype(bf16)
    bottom[0] = block[half:].astype(bf16)


def far_partials(places, tokens, cot, swapped):
    rows, width = cot.shape
    half = width // 2
    order = lambda i: 6 - 4 * i
    return pl.pallas_call(
        far_kernel,
        grid_spec=pltpu.PrefetchScalarGridSpec(
            num_scalar_prefetch=1,
            grid=(2,),
            in_specs=[
                pl.BlockSpec((rows, width), lambda i, p: (0, p[order(i)])),
                pl.BlockSpec((rows, width), lambda i, p: (0, 0)),
                pl.BlockSpec((1, rows, width), lambda i, p: (order(i), 0, 0)),
                pl.BlockSpec((1, rows, width), lambda i, p: (8, 0, 0)),
            ],
            out_specs=[pl.BlockSpec((1, half, width), lambda i, p: (i, 0, 0))] * 2,
        ),
        out_shape=[jax.ShapeDtypeStruct((2, half, width), bf16)] * 2,
        compiler_params=params(),
        cost_estimate=pl.CostEstimate(
            flops=2 * 4 * rows * width * width, bytes_accessed=10 * rows * width * 2, transcendentals=0
        ),
        name="far_partials",
    )(places, tokens, cot, swapped, swapped)


def near_kernel(places, tokens, cot, par, par_cot, out):
    out[0] = dot(tokens[...], cot[...], 0, 0) + dot(par[0], par_cot[0], 0, 0)


def near_partials(places, tokens, cot, swapped):
    rows, width = cot.shape

    def order(i):
        k = lax.rem(i, 3)
        return jnp.where(i < 3, 4, 0) + jnp.where(k == 0, 1, jnp.where(k == 1, 3, 0))

    return pl.pallas_call(
        near_kernel,
        grid_spec=pltpu.PrefetchScalarGridSpec(
            num_scalar_prefetch=1,
            grid=(6,),
            in_specs=[
                pl.BlockSpec((rows, width), lambda i, p: (0, p[order(i)])),
                pl.BlockSpec((rows, width), lambda i, p: (0, 0)),
                pl.BlockSpec((1, rows, width), lambda i, p: (order(i), 0, 0)),
                pl.BlockSpec((1, rows, width), lambda i, p: (8, 0, 0)),
            ],
            out_specs=pl.BlockSpec((1, width, width), lambda i, p: (i, 0, 0)),
        ),
        out_shape=jax.ShapeDtypeStruct((6, width, width), f32),
        compiler_params=params(),
        cost_estimate=pl.CostEstimate(
            flops=6 * 4 * rows * width * width,
            bytes_accessed=26 * rows * width * 2 + 6 * width * width * 4,
            transcendentals=0,
        ),
        name="near_partials",
    )(places, tokens, cot, swapped, swapped)


def relay_kernel(near, top, bottom, plus, minus):
    half = top.shape[1]
    plus[:half] = (near[0, :half] + top[0].astype(f32)).astype(bf16)
    plus[half:] = near[0, half:].astype(bf16)
    minus[:half] = near[1, :half].astype(bf16)
    minus[half:] = (near[1, half:] + bottom[0].astype(f32)).astype(bf16)


def relay(near, top, bottom, part):
    width = near.shape[1]
    half = width // 2
    return pl.pallas_call(
        relay_kernel,
        grid=(1,),
        in_specs=[
            pl.BlockSpec((3, width, width), lambda i: (part, 0, 0)),
            pl.BlockSpec((1, half, width), lambda i: (part, 0, 0)),
            pl.BlockSpec((1, half, width), lambda i: (part, 0, 0)),
        ],
        out_specs=[pl.BlockSpec((width, width), lambda i: (0, 0))] * 2,
        out_shape=[jax.ShapeDtypeStruct((width, width), bf16)] * 2,
        compiler_params=params(),
        cost_estimate=pl.CostEstimate(flops=width * width, bytes_accessed=7 * width * width * 2, transcendentals=0),
        name="relay",
    )(near, top, bottom)


def apply_kernel(first, places, tokens, par, cot, par_cot, w0, w1, w2a, w2b, w3, *rest):
    if first:
        v_own, v_par, grad, grad_par = rest
    else:
        v_own_in, v_par_in, _, v_own, v_par, grad, grad_par = rest
    step = pl.program_id(0)
    half = w2a.shape[0]

    @pl.when(step == 0)
    def _():
        if first:
            v_own[...] = jnp.zeros_like(v_own)
            v_par[...] = jnp.zeros_like(v_par)
        else:
            v_own[...] = v_own_in[...]
            v_par[...] = v_par_in[...]

    for k, w in ((0, w0), (1, w1), (3, w3)):

        @pl.when(step == k)
        def _(w=w):
            v_own[...] += dot(tokens[...], w[...], 1, 0)
            v_par[...] += dot(par[0], w[...], 1, 0)
            grad[...] = dot(cot[...], w[...], 1, 1).astype(bf16)
            grad_par[0] = dot(par_cot[0], w[...], 1, 1).astype(bf16)

    @pl.when(step == 2)
    def _():
        v_own[...] += dot(tokens[:, :half], w2a[...], 1, 0) + dot(tokens[:, half:], w2b[...], 1, 0)
        v_par[...] += dot(par[0, :, :half], w2a[...], 1, 0) + dot(par[0, :, half:], w2b[...], 1, 0)
        grad[:, :half] = dot(cot[...], w2a[...], 1, 1).astype(bf16)
        grad[:, half:] = dot(cot[...], w2b[...], 1, 1).astype(bf16)
        grad_par[0, :, :half] = dot(par_cot[0], w2a[...], 1, 1).astype(bf16)
        grad_par[0, :, half:] = dot(par_cot[0], w2b[...], 1, 1).astype(bf16)


def apply_weight(places, tokens, swapped, cot, pieces, carry, part):
    rows, width = cot.shape
    first = carry is None
    base = 4 * part
    full = lambda shape: pl.BlockSpec(shape, lambda i, p: (0,) * len(shape))
    v_spec = full((rows, width))
    grad_spec = pl.BlockSpec((rows, width), lambda i, p: (0, p[base + i]))
    in_specs = [
        pl.BlockSpec((rows, width), lambda i, p: (0, p[base + i])),
        pl.BlockSpec((1, rows, width), lambda i, p: (base + i, 0, 0)),
        full((rows, width)),
        pl.BlockSpec((1, rows, width), lambda i, p: (8, 0, 0)),
    ] + [full(w.shape) for w in pieces]
    operands = [places, tokens, swapped, cot, swapped, *pieces]
    aliases = {}
    if not first:
        aliases = {len(operands): 0, len(operands) + 1: 1, len(operands) + 2: 2}
        in_specs += [v_spec, v_spec, pl.BlockSpec(memory_space=pl.ANY)]
        operands += carry
    return pl.pallas_call(
        lambda *refs: apply_kernel(first, *refs),
        grid_spec=pltpu.PrefetchScalarGridSpec(
            num_scalar_prefetch=1,
            grid=(4,),
            in_specs=in_specs,
            out_specs=[v_spec, v_spec, grad_spec, pl.BlockSpec((1, rows, width), lambda i, p: (i, 0, 0))],
        ),
        out_shape=[
            jax.ShapeDtypeStruct((rows, width), f32),
            jax.ShapeDtypeStruct((rows, width), f32),
            jax.ShapeDtypeStruct(tokens.shape, bf16),
            jax.ShapeDtypeStruct((4, rows, width), bf16),
        ],
        input_output_aliases=aliases,
        compiler_params=params(),
        cost_estimate=pl.CostEstimate(
            flops=4 * 8 * rows * width * width,
            bytes_accessed=16 * rows * width * 2 + 4 * width * width * 2 + 8 * rows * width * 2,
            transcendentals=0,
        ),
        name="apply_weight",
    )(*operands)


def place_kernel(places, blocks, _, out):
    out[...] = blocks[0]


def place(places, blocks, whole, part):
    count, rows, width = blocks.shape
    return pl.pallas_call(
        place_kernel,
        grid_spec=pltpu.PrefetchScalarGridSpec(
            num_scalar_prefetch=1,
            grid=(count,),
            in_specs=[
                pl.BlockSpec((1, rows, width), lambda i, p: (i, 0, 0)),
                pl.BlockSpec(memory_space=pl.ANY),
            ],
            out_specs=pl.BlockSpec((rows, width), lambda i, p: (0, p[4 * part + i])),
        ),
        out_shape=jax.ShapeDtypeStruct(whole.shape, bf16),
        input_output_aliases={2: 0},
        compiler_params=params(),
        cost_estimate=pl.CostEstimate(flops=0, bytes_accessed=2 * count * rows * width * 2, transcendentals=0),
        name="place",
    )(places, blocks, whole)


def gather_pieces(shard):
    half = shard.shape[0] // 2
    behind = send(shard, PLUS)
    ahead = send(shard, MINUS)
    far_top = send(behind[:half], PLUS)
    far_bottom = send(ahead[half:], MINUS)
    return (shard, ahead, far_top, far_bottom, behind)


def replica_sum(part):
    for bit in (1, 2, 4, 8):
        part = part + lax.ppermute(part, "replica", [(i, i ^ bit) for i in range(16)])
    return part


def nesterov(averaged, moment, global_part):
    moment_next = momentum_decay * moment + averaged
    global_next = global_part - outer_rate * (averaged + momentum_decay * moment_next)
    return (global_next, moment_next)


def body(
    tokens, cotangent, w_value, outer_global, outer_momentum, local_params, outer_delta, fragment
):
    me = lax.axis_index("fsdp")
    core, x, z = lax.rem(me, NC), lax.rem(me // NC, NX), me // (NC * NX)
    steps = jnp.arange(8, dtype=jnp.int32)
    chips = lax.rem(z + steps // NX, NZ) * NX + lax.rem(x + steps, NX)
    own = chips * NC + core
    other = chips * NC + (1 - core)

    shard = w_value[0]
    shard_across = send(shard, ACROSS)
    pieces = gather_pieces(shard)
    outgoing = select(jnp.concatenate([other, other[:1]]), tokens, cotangent)
    swapped = send(outgoing, OTHER_CORE)

    top, bottom = far_partials(own, tokens, cotangent, swapped)
    top, bottom = send(top, PLUS), send(bottom, MINUS)
    near = near_partials(own, tokens, cotangent, swapped)
    plus, minus = relay(near, top, bottom, 0)
    from_left, from_right = send(plus, PLUS), send(minus, MINUS)
    across = (near[2] + from_left.astype(f32) + from_right.astype(f32)).astype(bf16)
    from_across = send(across, ACROSS)

    v_own, v_par, grad, grad_par = apply_weight(own, tokens, swapped, cotangent, pieces, None, 0)
    grad_back = send(grad_par, OTHER_CORE)

    pieces = gather_pieces(shard_across)
    plus, minus = relay(near, top, bottom, 1)
    from_left, from_right = send(plus, PLUS), send(minus, MINUS)

    grad = place(other, grad_back, grad, 0)
    v_own, v_par, grad, grad_par = apply_weight(
        own, tokens, swapped, cotangent, pieces, [v_own, v_par, grad], 1
    )
    v_back = send(v_par, OTHER_CORE)
    grad = place(other, send(grad_par, OTHER_CORE), grad, 1)
    values = (v_own + v_back).astype(bf16)
    grad_weight = (
        near[5] + from_left.astype(f32) + from_right.astype(f32) + from_across.astype(f32)
    )

    fragment_id = fragment[0]
    chosen_global = lax.dynamic_index_in_dim(outer_global, fragment_id, 0, keepdims=False)
    chosen_moment = lax.dynamic_index_in_dim(outer_momentum, fragment_id, 0, keepdims=False)
    chosen_local = lax.dynamic_index_in_dim(local_params[0], fragment_id, 0, keepdims=False)
    replicas = lax.axis_size("replica")
    summed = replica_sum(outer_delta[0])
    new_global, new_momentum = nesterov(summed / replicas, chosen_moment, chosen_global)
    new_local = mix_weight * chosen_local + (1.0 - mix_weight) * new_global
    return (values, grad, grad_weight[None], new_global, new_momentum, new_local[None])


def solution(mesh):
    in_specs = (
        P(("replica", "fsdp"), None),
        P(("replica", "fsdp"), None),
        P("replica", "fsdp", None),
        P(None, "fsdp", None),
        P(None, "fsdp", None),
        P("replica", None, "fsdp", None),
        P("replica", "fsdp", None),
        P(),
    )
    out_specs = (
        P(("replica", "fsdp"), None),
        P(("replica", "fsdp"), None),
        P("replica", "fsdp", None),
        P("fsdp", None),
        P("fsdp", None),
        P("replica", "fsdp", None),
    )
    return jax.shard_map(body, mesh=mesh, in_specs=in_specs, out_specs=out_specs, check_vma=False)
```

```python
import jax
import jax.numpy as jnp
from jax import lax
from jax.experimental import pallas as pl
from jax.experimental.pallas import tpu as pltpu
from jax.sharding import PartitionSpec as P

outer_rate = 0.7
momentum_decay = 0.9
mix_weight = 0.5

f32, bf16 = jnp.float32, jnp.bfloat16
NX, NZ, NC = 4, 2, 2
CUT = 256
HOLD = 14
WHOLE = pl.BlockSpec(memory_space=pltpu.VMEM)
FAR = pl.BlockSpec(memory_space=pltpu.HBM)
INDEX = pl.BlockSpec(memory_space=pltpu.SMEM)
DMAS = pltpu.SemaphoreType.DMA


def fsdp_perm(dz, dx, dc):
    pairs = []
    for z in range(NZ):
        for x in range(NX):
            for c in range(NC):
                there = (((z + dz) % NZ) * NX + (x + dx) % NX) * NC + (c + dc) % NC
                pairs.append(((z * NX + x) * NC + c, there))
    return pairs


PLUS, MINUS = fsdp_perm(0, 1, 0), fsdp_perm(0, -1, 0)
ACROSS, OTHER_CORE, DIAGONAL = fsdp_perm(1, 0, 0), fsdp_perm(0, 0, 1), fsdp_perm(1, 0, 1)


def send(array, pairs):
    return lax.ppermute(array, "fsdp", pairs)


def after(value, *earlier):
    return lax.optimization_barrier((value, *earlier))[0]


def call(kernel, name, in_specs, out_specs, out_shape, operands, scratch=(), aliases={}, limit=16, traffic=2):
    return pl.pallas_call(
        kernel,
        in_specs=in_specs,
        out_specs=out_specs,
        out_shape=out_shape,
        scratch_shapes=scratch,
        input_output_aliases=aliases,
        compiler_params=pltpu.CompilerParams(vmem_limit_bytes=limit * 1024 * 1024),
        cost_estimate=pl.CostEstimate(flops=0, bytes_accessed=traffic * 1024 * 1024, transcendentals=0),
        name=name,
    )(*operands)


def dot(a, b, ca, cb):
    return lax.dot_general(a, b, (((ca,), (cb,)), ((), ())), preferred_element_type=f32)


def columns(whole, place, width):
    return whole.at[:, pl.ds(pl.multiple_of(place * width, width), width)]


FIRST, SECOND = (6, 2), (4, 5, 7, 0, 1, 3)


def select_kernel(places, tokens, cot, first, second, sems):
    width = cot.shape[1]
    copies = [pltpu.make_async_copy(cot, first.at[len(FIRST)], sems.at[8])]
    for out, blocks in ((first, FIRST), (second, SECOND)):
        for i, b in enumerate(blocks):
            copies.append(pltpu.make_async_copy(columns(tokens, places[b], width), out.at[i], sems.at[b]))
    for copy in copies:
        copy.start()
    for copy in copies:
        copy.wait()


def select(places, tokens, cot):
    return call(
        select_kernel,
        "select",
        [INDEX, WHOLE, WHOLE],
        [WHOLE] * 2,
        [jax.ShapeDtypeStruct((count, *cot.shape), bf16) for count in (len(FIRST) + 1, len(SECOND))],
        (places, tokens, cot),
        [DMAS((9,))],
        traffic=4,
    )


def block_of(tokens, place, width):
    return tokens[:, pl.ds(pl.multiple_of(place * width, width), width)]


def partner_block(par, b):
    first, second = par
    return first[FIRST.index(b)] if b in FIRST else second[SECOND.index(b)]


def partial(b, places, tokens, cot, *par):
    own = block_of(tokens, places[b], cot.shape[1])
    return dot(own, cot[...], 0, 0) + dot(partner_block(par, b), par[0][len(FIRST)], 0, 0)


ROWS = [INDEX] + [WHOLE] * 4


def far_kernel(*refs):
    *rows, top, bottom = refs
    half = top.shape[1]
    for i, b in enumerate((6, 2)):
        block = partial(b, *rows)
        top[i] = block[:half].astype(bf16)
        bottom[i] = block[half:].astype(bf16)


def far_partials(*rows):
    width = rows[2].shape[1]
    return call(
        far_kernel,
        "far_partials",
        ROWS,
        [WHOLE] * 2,
        [jax.ShapeDtypeStruct((2, width // 2, width), bf16)] * 2,
        rows,
        traffic=5,
    )


def relay_kernel(part, *refs):
    rows, (top, bottom), outs = refs[:5], refs[5:7], refs[7:]
    plus, minus = outs[: len(outs) // 2], outs[len(outs) // 2 :]
    half = top.shape[1]
    for k, pieces, arrived, at in ((1, plus, top, 0), (3, minus, bottom, half)):
        block = partial(4 - 4 * part + k, *rows)
        row = 0
        for piece in pieces:
            count = piece.shape[0]
            low, high = max(row, at), min(row + count, at + half)
            if row < low:
                piece[: min(low - row, count)] = block[row : min(low, row + count)].astype(bf16)
            if low < high:
                mine = arrived[part, low - at : high - at].astype(f32)
                piece[low - row : high - row] = (block[low:high] + mine).astype(bf16)
            if max(high, row) < row + count and low < row + count:
                start = max(high, row)
                piece[start - row :] = block[start : row + count].astype(bf16)
            row += count


def relay(rows, top, bottom, part, cuts):
    width = rows[2].shape[1]
    return call(
        lambda *refs: relay_kernel(part, *refs),
        "relay",
        ROWS + [WHOLE] * 2,
        [WHOLE] * (2 * len(cuts)),
        [jax.ShapeDtypeStruct((count, width), bf16) for count in cuts] * 2,
        (*rows, top, bottom),
        traffic=5,
    )


def closing_kernel(part, *refs):
    rows, arrived, out = refs[:5], refs[5:-1], refs[-1]
    total = partial(4 - 4 * part, *rows)
    if part:
        total += arrived[0][...].astype(f32)
        arrived = arrived[1:]
    row = 0
    for left, right in zip(arrived[::2], arrived[1::2]):
        at = slice(row, row + left.shape[0])
        out[at] = (total[at] + left[...].astype(f32) + right[...].astype(f32)).astype(out.dtype)
        row += left.shape[0]


def closing(rows, arrived, part, dtype):
    width = rows[2].shape[1]
    return call(
        lambda *refs: closing_kernel(part, *refs),
        "closing",
        ROWS + [WHOLE] * len(arrived),
        WHOLE,
        jax.ShapeDtypeStruct((width, width), dtype),
        (*rows, *arrived),
        traffic=4,
    )


def apply_kernel(part, *refs):
    rows, (w0, w1, w2a, w2b, w3), rest = refs[:5], refs[5:10], refs[10:]
    places, tokens, cot, *par = rows
    if part:
        v_own_in, v_par_in, _, v_own, grad, *back, ready, sems = rest
    else:
        v_own, v_par, grad, *back, ready, sems = rest
    par_cot = par[0].at[len(FIRST)]
    width = cot.shape[1]
    half = w2a.shape[0]
    copies = []
    sums = [v_own_in[...], v_par_in[...]] if part else [0.0, 0.0]
    for k, w in enumerate((w0, w1, None, w3)):
        pieces = [(w, slice(0, width))] if k != 2 else [(w2a, slice(0, half)), (w2b, slice(half, width))]
        b = 4 * part + k
        blocks = (block_of(tokens, places[b], width), partner_block(par, b))
        for n, block in enumerate(blocks):
            sums[n] += sum(dot(block[:, s], p[...], 1, 0) for p, s in pieces)
        for p, s in pieces:
            ready[k, :, s] = dot(cot[...], p[...], 1, 1).astype(bf16)
            returned = dot(par_cot[...], p[...], 1, 1).astype(bf16)
            if part:
                back[k][: returned.shape[0], s] = returned
            else:
                back[k // 2][k % 2, :, s] = returned
        copy = pltpu.make_async_copy(ready.at[k], columns(grad, places[b], width), sems.at[k])
        copy.start()
        copies.append(copy)
    v_own[...] = sums[0]
    if part:
        rows_each = cot.shape[0] // 4
        for k in range(4):
            back[k][cot.shape[0] :] = sums[1][k * rows_each : (k + 1) * rows_each].astype(bf16)
    else:
        v_par[...] = sums[1]
    for copy in copies:
        copy.wait()


def apply_weight(rows, pieces, carry, part):
    tokens, cot = rows[1:3]
    operands = (*rows, *pieces, *carry)
    total = jax.ShapeDtypeStruct(cot.shape, f32)
    whole = jax.ShapeDtypeStruct(tokens.shape, bf16)
    count, width = cot.shape
    shapes = [(count + count // 4, width)] * 4 if part else [(2, count, width)] * 2
    back = [jax.ShapeDtypeStruct(shape, bf16) for shape in shapes]
    return call(
        lambda *refs: apply_kernel(part, *refs),
        "apply_weight",
        ROWS + [WHOLE] * 5 + ([WHOLE, WHOLE, FAR] if part else []),
        [WHOLE] * (2 - part) + [FAR] + [WHOLE] * len(back),
        [total] * (2 - part) + [whole] + back,
        operands,
        [pltpu.VMEM((4, *cot.shape), bf16), DMAS((4,))],
        {len(operands) - 1: 1} if part else {},
        traffic=4,
    )


def place_kernel(part, places, *rest):
    if part:
        *blocks, v_own, _, out, values, sems = rest
        count = v_own.shape[0]
        sources = [block.at[pl.ds(0, count)] for block in blocks]
    else:
        *blocks, _, out, sems = rest
        sources = [block.at[k] for block in blocks for k in range(2)]
    width = sources[0].shape[-1]
    copies = [
        pltpu.make_async_copy(source, columns(out, places[4 * part + k], width), sems.at[k])
        for k, source in enumerate(sources)
    ]
    for copy in copies:
        copy.start()
    if part:
        for k, block in enumerate(blocks):
            at = slice(k * count // 4, (k + 1) * count // 4)
            values[at] = (v_own[at] + block[count:].astype(f32)).astype(bf16)
    for copy in copies:
        copy.wait()


def place(places, blocks, whole, v_own, part):
    operands = (places, *blocks, v_own, whole) if part else (places, *blocks, whole)
    out = jax.ShapeDtypeStruct(whole.shape, bf16)
    return call(
        lambda *refs: place_kernel(part, *refs),
        "place",
        [INDEX] + [WHOLE] * (len(operands) - 2) + [FAR],
        [FAR, WHOLE] if part else FAR,
        [out, jax.ShapeDtypeStruct(v_own.shape, bf16)] if part else out,
        operands,
        [DMAS((4,))],
        {len(operands) - 1: 0},
        traffic=5,
    )


def partner(part, bits):
    return lax.ppermute(part, "replica", [(i, i ^ bits) for i in range(16)])


def outer_kernel(fragment, delta, moment, whole, local, new_global, new_moment, new_local):
    averaged = delta[...] / 16.0
    moment_next = momentum_decay * moment[0] + averaged
    global_next = whole[0] - outer_rate * (averaged + momentum_decay * moment_next)
    new_moment[...] = moment_next
    new_global[...] = global_next
    new_local[0] = mix_weight * local[0, 0] + (1.0 - mix_weight) * global_next


def outer_step(fragment, delta, moment, whole, local):
    rows, width = delta.shape
    flat = pl.BlockSpec((rows, width), lambda i, f: (0, 0))
    chosen = pl.BlockSpec((1, rows, width), lambda i, f: (f[0], 0, 0))
    return pl.pallas_call(
        outer_kernel,
        grid_spec=pltpu.PrefetchScalarGridSpec(
            num_scalar_prefetch=1,
            grid=(1,),
            in_specs=[flat, chosen, chosen, pl.BlockSpec((1, 1, rows, width), lambda i, f: (0, f[0], 0, 0))],
            out_specs=[flat, flat, pl.BlockSpec((1, rows, width), lambda i, f: (0, 0, 0))],
        ),
        out_shape=[jax.ShapeDtypeStruct((rows, width), f32)] * 2 + [jax.ShapeDtypeStruct((1, rows, width), f32)],
        compiler_params=pltpu.CompilerParams(vmem_limit_bytes=8 * 1024 * 1024),
        cost_estimate=pl.CostEstimate(flops=0, bytes_accessed=1024 * 1024, transcendentals=0),
        name="outer_step",
    )(fragment, delta, moment, whole, local)


def hold_kernel(places, _, out):
    for b in range(8):
        out[b] = places[b]


def hold(places, array, traffic):
    return call(
        hold_kernel,
        "hold",
        [INDEX, FAR],
        INDEX,
        jax.ShapeDtypeStruct(places.shape, places.dtype),
        (places, array),
        traffic=traffic,
    )


def body(
    tokens, cotangent, w_value, outer_global, outer_momentum, local_params, outer_delta, fragment
):
    me = lax.axis_index("fsdp")
    core, x, z = lax.rem(me, NC), lax.rem(me // NC, NX), me // (NC * NX)
    steps = jnp.arange(8, dtype=jnp.int32)
    chips = lax.rem(z + steps // NX, NZ) * NX + lax.rem(x + steps, NX)
    own = chips * NC + core
    other = chips * NC + (1 - core)

    shard = w_value[0]
    width = shard.shape[1]
    half = shard.shape[0] // 2
    par = [send(piece, OTHER_CORE) for piece in select(other, tokens, cotangent)]
    behind, ahead = send(shard, PLUS), send(shard, MINUS)
    shard_across = send(shard, ACROSS)

    rows = (own, tokens, cotangent, *par)
    top, bottom = far_partials(*rows)
    delta = after(outer_delta[0], top)
    delta = delta + partner(delta, 1)
    top, bottom = send(top, PLUS), send(bottom, MINUS)
    far_top = send(after(behind[:half], delta), PLUS)
    far_bottom = send(after(ahead[half:], delta), MINUS)

    across_in = hold(own, shard_across, HOLD)
    top, bottom, far_top, far_bottom = lax.optimization_barrier((top, bottom, far_top, far_bottom))
    plus, minus = relay((across_in, *rows[1:]), top, bottom, 0, (width,))
    from_left, from_right = send(plus, PLUS), send(minus, MINUS)
    delta = after(delta, plus)
    delta = sum((partner(delta, bits) for bits in (4, 8, 12)), delta)
    pieces = (shard, ahead, after(far_top, delta), far_bottom, behind)
    v_own, v_par, grad, *back = apply_weight(rows, pieces, (), 0)
    back = [send(piece, OTHER_CORE) for piece in back]

    shard_across = after(shard_across, from_left, from_right, v_own, across_in)
    behind, ahead = send(shard_across, PLUS), send(shard_across, MINUS)
    across = closing((across_in, *rows[1:]), (from_left, from_right), 0, bf16)
    from_across = send(across, ACROSS)
    delta = delta + partner(after(delta, v_own), 2)
    plus, plus_late, minus, minus_late = relay(rows, after(top, across), bottom, 1, (CUT, width - CUT))
    grad = place(other, back, grad, None, 0)

    far_top, far_bottom = send(behind[:half], PLUS), send(ahead[half:], MINUS)
    left, right = send(after(plus, behind), PLUS), send(after(minus, ahead, grad), MINUS)
    pieces = (shard_across, ahead, far_top, far_bottom, behind)
    v_own, grad, *back = apply_weight(rows, pieces, (v_own, v_par, grad), 1)
    everything = (v_own, from_across, delta, left, right)
    left_late = send(after(plus_late, *everything), PLUS)
    right_late = send(after(minus_late, *everything), MINUS)
    back = [send(piece, OTHER_CORE) for piece in back]
    grad, values = place(other, back, grad, v_own, 1)
    rows = (after(own, grad, values), *rows[1:])
    grad_weight = closing(rows, (from_across, left, right, left_late, right_late), 1, f32)

    new_global, new_momentum, new_local = outer_step(
        fragment, delta, outer_momentum, outer_global, local_params
    )
    return (values, grad, grad_weight[None], new_global, new_momentum, new_local)


def solution(mesh):
    in_specs = (
        P(("replica", "fsdp"), None),
        P(("replica", "fsdp"), None),
        P("replica", "fsdp", None),
        P(None, "fsdp", None),
        P(None, "fsdp", None),
        P("replica", None, "fsdp", None),
        P("replica", "fsdp", None),
        P(),
    )
    out_specs = (
        P(("replica", "fsdp"), None),
        P(("replica", "fsdp"), None),
        P("replica", "fsdp", None),
        P("fsdp", None),
        P("fsdp", None),
        P("replica", "fsdp", None),
    )
    return jax.shard_map(body, mesh=mesh, in_specs=in_specs, out_specs=out_specs, check_vma=False)
```

```python
import jax
import jax.numpy as jnp
from jax import lax
from jax.experimental import pallas as pl
from jax.experimental.pallas import tpu as pltpu
from jax.sharding import PartitionSpec as P

outer_rate = 0.7
momentum_decay = 0.9
mix_weight = 0.5

f32, bf16 = jnp.float32, jnp.bfloat16
NX, NZ, NC = 4, 2, 2
CUT = 256
HOLD = 14
WHOLE = pl.BlockSpec(memory_space=pltpu.VMEM)
FAR = pl.BlockSpec(memory_space=pltpu.HBM)
INDEX = pl.BlockSpec(memory_space=pltpu.SMEM)
DMAS = pltpu.SemaphoreType.DMA


def fsdp_perm(dz, dx, dc):
    pairs = []
    for z in range(NZ):
        for x in range(NX):
            for c in range(NC):
                there = (((z + dz) % NZ) * NX + (x + dx) % NX) * NC + (c + dc) % NC
                pairs.append(((z * NX + x) * NC + c, there))
    return pairs


PLUS, MINUS = fsdp_perm(0, 1, 0), fsdp_perm(0, -1, 0)
ACROSS, OTHER_CORE, DIAGONAL = fsdp_perm(1, 0, 0), fsdp_perm(0, 0, 1), fsdp_perm(1, 0, 1)


def send(array, pairs):
    return lax.ppermute(array, "fsdp", pairs)


def after(value, *earlier):
    return lax.optimization_barrier((value, *earlier))[0]


def call(kernel, name, in_specs, out_specs, out_shape, operands, scratch=(), aliases={}, limit=16, traffic=2):
    return pl.pallas_call(
        kernel,
        in_specs=in_specs,
        out_specs=out_specs,
        out_shape=out_shape,
        scratch_shapes=scratch,
        input_output_aliases=aliases,
        compiler_params=pltpu.CompilerParams(vmem_limit_bytes=limit * 1024 * 1024),
        cost_estimate=pl.CostEstimate(flops=0, bytes_accessed=traffic * 1024 * 1024, transcendentals=0),
        name=name,
    )(*operands)


def dot(a, b, ca, cb):
    return lax.dot_general(a, b, (((ca,), (cb,)), ((), ())), preferred_element_type=f32)


def columns(whole, place, width):
    return whole.at[:, pl.ds(pl.multiple_of(place * width, width), width)]


FIRST, SECOND = (6, 2), (4, 5, 7, 0, 1, 3)


def select_kernel(places, tokens, cot, first, second, sems):
    width = cot.shape[1]
    copies = [pltpu.make_async_copy(cot, first.at[len(FIRST)], sems.at[8])]
    for out, blocks in ((first, FIRST), (second, SECOND)):
        for i, b in enumerate(blocks):
            copies.append(pltpu.make_async_copy(columns(tokens, places[b], width), out.at[i], sems.at[b]))
    for copy in copies:
        copy.start()
    for copy in copies:
        copy.wait()


def select(places, tokens, cot):
    return call(
        select_kernel,
        "select",
        [INDEX, WHOLE, WHOLE],
        [WHOLE] * 2,
        [jax.ShapeDtypeStruct((count, *cot.shape), bf16) for count in (len(FIRST) + 1, len(SECOND))],
        (places, tokens, cot),
        [DMAS((9,))],
        traffic=4,
    )


def block_of(tokens, place, width):
    return tokens[:, pl.ds(pl.multiple_of(place * width, width), width)]


def partner_block(par, b):
    first, second = par
    return first[FIRST.index(b)] if b in FIRST else second[SECOND.index(b)]


def partial(b, places, tokens, cot, *par):
    own = block_of(tokens, places[b], cot.shape[1])
    return dot(own, cot[...], 0, 0) + dot(partner_block(par, b), par[0][len(FIRST)], 0, 0)


ROWS = [INDEX] + [WHOLE] * 4


def far_kernel(*refs):
    *rows, top, bottom = refs
    half = top.shape[1]
    for i, b in enumerate((6, 2)):
        block = partial(b, *rows)
        top[i] = block[:half].astype(bf16)
        bottom[i] = block[half:].astype(bf16)


def far_partials(*rows):
    width = rows[2].shape[1]
    return call(
        far_kernel,
        "far_partials",
        ROWS,
        [WHOLE] * 2,
        [jax.ShapeDtypeStruct((2, width // 2, width), bf16)] * 2,
        rows,
        traffic=5,
    )


def relay_kernel(part, *refs):
    rows, (top, bottom), outs = refs[:5], refs[5:7], refs[7:]
    plus, minus = outs[: len(outs) // 2], outs[len(outs) // 2 :]
    half = top.shape[1]
    for k, pieces, arrived, at in ((1, plus, top, 0), (3, minus, bottom, half)):
        block = partial(4 - 4 * part + k, *rows)
        row = 0
        for piece in pieces:
            count = piece.shape[0]
            low, high = max(row, at), min(row + count, at + half)
            if row < low:
                piece[: min(low - row, count)] = block[row : min(low, row + count)].astype(bf16)
            if low < high:
                mine = arrived[part, low - at : high - at].astype(f32)
                piece[low - row : high - row] = (block[low:high] + mine).astype(bf16)
            if max(high, row) < row + count and low < row + count:
                start = max(high, row)
                piece[start - row :] = block[start : row + count].astype(bf16)
            row += count


def relay(rows, top, bottom, part, cuts):
    width = rows[2].shape[1]
    return call(
        lambda *refs: relay_kernel(part, *refs),
        "relay",
        ROWS + [WHOLE] * 2,
        [WHOLE] * (2 * len(cuts)),
        [jax.ShapeDtypeStruct((count, width), bf16) for count in cuts] * 2,
        (*rows, top, bottom),
        traffic=5,
    )


def closing_kernel(part, *refs):
    *rows, left, right, out = refs
    total = partial(4 - 4 * part, *rows)
    count = left.shape[0]
    added = total[:count] + left[...].astype(f32) + right[...].astype(f32)
    out[:count] = added.astype(out.dtype)
    if count < out.shape[0]:
        out[count:] = total[count:].astype(out.dtype)


def closing(rows, left, right, part):
    width = rows[2].shape[1]
    return call(
        lambda *refs: closing_kernel(part, *refs),
        "closing",
        ROWS + [WHOLE] * 2,
        WHOLE,
        jax.ShapeDtypeStruct((width, width), f32 if part else bf16),
        (*rows, left, right),
        traffic=4,
    )


def finish_kernel(total, across, left, right, out):
    out[:CUT] = total[:CUT] + across[:CUT].astype(f32)
    late = left[...].astype(f32) + right[...].astype(f32)
    out[CUT:] = total[CUT:] + across[CUT:].astype(f32) + late


def finish(total, across, left, right):
    return call(
        finish_kernel,
        "finish",
        [WHOLE] * 4,
        WHOLE,
        jax.ShapeDtypeStruct(total.shape, f32),
        (total, across, left, right),
    )


def apply_kernel(part, *refs):
    rows, (w0, w1, w2a, w2b, w3), rest = refs[:5], refs[5:10], refs[10:]
    places, tokens, cot, *par = rows
    if part:
        v_own_in, v_par_in, _, v_own, grad, *back, ready, sems = rest
    else:
        v_own, v_par, grad, *back, ready, sems = rest
    par_cot = par[0].at[len(FIRST)]
    width = cot.shape[1]
    half = w2a.shape[0]
    copies = []
    sums = [v_own_in[...], v_par_in[...]] if part else [0.0, 0.0]
    for k, w in enumerate((w0, w1, None, w3)):
        pieces = [(w, slice(0, width))] if k != 2 else [(w2a, slice(0, half)), (w2b, slice(half, width))]
        b = 4 * part + k
        blocks = (block_of(tokens, places[b], width), partner_block(par, b))
        for n, block in enumerate(blocks):
            sums[n] += sum(dot(block[:, s], p[...], 1, 0) for p, s in pieces)
        for p, s in pieces:
            ready[k, :, s] = dot(cot[...], p[...], 1, 1).astype(bf16)
            returned = dot(par_cot[...], p[...], 1, 1).astype(bf16)
            if part:
                back[k][: returned.shape[0], s] = returned
            else:
                back[k // 2][k % 2, :, s] = returned
        copy = pltpu.make_async_copy(ready.at[k], columns(grad, places[b], width), sems.at[k])
        copy.start()
        copies.append(copy)
    v_own[...] = sums[0]
    if part:
        rows_each = cot.shape[0] // 4
        for k in range(4):
            back[k][cot.shape[0] :] = sums[1][k * rows_each : (k + 1) * rows_each].astype(bf16)
    else:
        v_par[...] = sums[1]
    for copy in copies:
        copy.wait()


def apply_weight(rows, pieces, carry, part):
    tokens, cot = rows[1:3]
    operands = (*rows, *pieces, *carry)
    total = jax.ShapeDtypeStruct(cot.shape, f32)
    whole = jax.ShapeDtypeStruct(tokens.shape, bf16)
    count, width = cot.shape
    shapes = [(count + count // 4, width)] * 4 if part else [(2, count, width)] * 2
    back = [jax.ShapeDtypeStruct(shape, bf16) for shape in shapes]
    return call(
        lambda *refs: apply_kernel(part, *refs),
        "apply_weight",
        ROWS + [WHOLE] * 5 + ([WHOLE, WHOLE, FAR] if part else []),
        [WHOLE] * (2 - part) + [FAR] + [WHOLE] * len(back),
        [total] * (2 - part) + [whole] + back,
        operands,
        [pltpu.VMEM((4, *cot.shape), bf16), DMAS((4,))],
        {len(operands) - 1: 1} if part else {},
        traffic=4,
    )


def place_kernel(part, places, *rest):
    if part:
        *blocks, v_own, _, out, values, sems = rest
        count = v_own.shape[0]
        sources = [block.at[pl.ds(0, count)] for block in blocks]
    else:
        *blocks, _, out, sems = rest
        sources = [block.at[k] for block in blocks for k in range(2)]
    width = sources[0].shape[-1]
    copies = [
        pltpu.make_async_copy(source, columns(out, places[4 * part + k], width), sems.at[k])
        for k, source in enumerate(sources)
    ]
    for copy in copies:
        copy.start()
    if part:
        for k, block in enumerate(blocks):
            at = slice(k * count // 4, (k + 1) * count // 4)
            values[at] = (v_own[at] + block[count:].astype(f32)).astype(bf16)
    for copy in copies:
        copy.wait()


def place(places, blocks, whole, v_own, part):
    operands = (places, *blocks, v_own, whole) if part else (places, *blocks, whole)
    out = jax.ShapeDtypeStruct(whole.shape, bf16)
    return call(
        lambda *refs: place_kernel(part, *refs),
        "place",
        [INDEX] + [WHOLE] * (len(operands) - 2) + [FAR],
        [FAR, WHOLE] if part else FAR,
        [out, jax.ShapeDtypeStruct(v_own.shape, bf16)] if part else out,
        operands,
        [DMAS((4,))],
        {len(operands) - 1: 0},
        traffic=5,
    )


def partner(part, bits):
    return lax.ppermute(part, "replica", [(i, i ^ bits) for i in range(16)])


def outer_kernel(fragment, delta, moment, whole, local, new_global, new_moment, new_local):
    averaged = delta[...] / 16.0
    moment_next = momentum_decay * moment[0] + averaged
    global_next = whole[0] - outer_rate * (averaged + momentum_decay * moment_next)
    new_moment[...] = moment_next
    new_global[...] = global_next
    new_local[0] = mix_weight * local[0, 0] + (1.0 - mix_weight) * global_next


def outer_step(fragment, delta, moment, whole, local):
    rows, width = delta.shape
    flat = pl.BlockSpec((rows, width), lambda i, f: (0, 0))
    chosen = pl.BlockSpec((1, rows, width), lambda i, f: (f[0], 0, 0))
    return pl.pallas_call(
        outer_kernel,
        grid_spec=pltpu.PrefetchScalarGridSpec(
            num_scalar_prefetch=1,
            grid=(1,),
            in_specs=[flat, chosen, chosen, pl.BlockSpec((1, 1, rows, width), lambda i, f: (0, f[0], 0, 0))],
            out_specs=[flat, flat, pl.BlockSpec((1, rows, width), lambda i, f: (0, 0, 0))],
        ),
        out_shape=[jax.ShapeDtypeStruct((rows, width), f32)] * 2 + [jax.ShapeDtypeStruct((1, rows, width), f32)],
        compiler_params=pltpu.CompilerParams(vmem_limit_bytes=8 * 1024 * 1024),
        cost_estimate=pl.CostEstimate(flops=0, bytes_accessed=1024 * 1024, transcendentals=0),
        name="outer_step",
    )(fragment, delta, moment, whole, local)


def hold_kernel(places, _, out):
    for b in range(8):
        out[b] = places[b]


def hold(places, array, traffic):
    return call(
        hold_kernel,
        "hold",
        [INDEX, FAR],
        INDEX,
        jax.ShapeDtypeStruct(places.shape, places.dtype),
        (places, array),
        traffic=traffic,
    )


def body(
    tokens, cotangent, w_value, outer_global, outer_momentum, local_params, outer_delta, fragment
):
    me = lax.axis_index("fsdp")
    core, x, z = lax.rem(me, NC), lax.rem(me // NC, NX), me // (NC * NX)
    steps = jnp.arange(8, dtype=jnp.int32)
    chips = lax.rem(z + steps // NX, NZ) * NX + lax.rem(x + steps, NX)
    own = chips * NC + core
    other = chips * NC + (1 - core)

    shard = w_value[0]
    width = shard.shape[1]
    half = shard.shape[0] // 2
    par = [send(piece, OTHER_CORE) for piece in select(other, tokens, cotangent)]
    behind, ahead = send(shard, PLUS), send(shard, MINUS)
    shard_across = send(shard, ACROSS)

    rows = (own, tokens, cotangent, *par)
    top, bottom = far_partials(*rows)
    delta = after(outer_delta[0], top)
    delta = delta + partner(delta, 1)
    top, bottom = send(top, PLUS), send(bottom, MINUS)
    far_top = send(after(behind[:half], delta), PLUS)
    far_bottom = send(after(ahead[half:], delta), MINUS)

    across_in = hold(own, shard_across, HOLD)
    top, bottom, far_top, far_bottom = lax.optimization_barrier((top, bottom, far_top, far_bottom))
    plus, minus = relay((across_in, *rows[1:]), top, bottom, 0, (width,))
    from_left, from_right = send(plus, PLUS), send(minus, MINUS)
    delta = after(delta, plus)
    delta = sum((partner(delta, bits) for bits in (4, 8, 12)), delta)
    pieces = (shard, ahead, after(far_top, delta), far_bottom, behind)
    v_own, v_par, grad, *back = apply_weight(rows, pieces, (), 0)
    back = [send(piece, OTHER_CORE) for piece in back]

    shard_across = after(shard_across, from_left, from_right, v_own, across_in)
    behind, ahead = send(shard_across, PLUS), send(shard_across, MINUS)
    across = closing((across_in, *rows[1:]), from_left, from_right, 0)
    from_across = send(across, ACROSS)
    delta = delta + partner(after(delta, v_own), 2)
    plus, plus_late, minus, minus_late = relay(rows, after(top, across), bottom, 1, (CUT, width - CUT))
    grad = place(other, back, grad, None, 0)

    far_top, far_bottom = send(behind[:half], PLUS), send(ahead[half:], MINUS)
    left, right = send(after(plus, behind), PLUS), send(after(minus, ahead, grad), MINUS)
    pieces = (shard_across, ahead, far_top, far_bottom, behind)
    v_own, grad, *back = apply_weight(rows, pieces, (v_own, v_par, grad), 1)
    everything = (v_own, from_across, delta, left, right)
    left_late = send(after(plus_late, *everything), PLUS)
    right_late = send(after(minus_late, *everything), MINUS)
    back = [send(piece, OTHER_CORE) for piece in back]
    total = closing(rows, left, right, 1)
    grad, values = place(after(other, total), back, grad, v_own, 1)
    grad_weight = finish(after(total, grad, values), from_across, left_late, right_late)

    new_global, new_momentum, new_local = outer_step(
        fragment, delta, outer_momentum, outer_global, local_params
    )
    return (values, grad, grad_weight[None], new_global, new_momentum, new_local)


def solution(mesh):
    in_specs = (
        P(("replica", "fsdp"), None),
        P(("replica", "fsdp"), None),
        P("replica", "fsdp", None),
        P(None, "fsdp", None),
        P(None, "fsdp", None),
        P("replica", None, "fsdp", None),
        P("replica", "fsdp", None),
        P(),
    )
    out_specs = (
        P(("replica", "fsdp"), None),
        P(("replica", "fsdp"), None),
        P("replica", "fsdp", None),
        P("fsdp", None),
        P("fsdp", None),
        P("replica", "fsdp", None),
    )
    return jax.shard_map(body, mesh=mesh, in_specs=in_specs, out_specs=out_specs, check_vma=False)
```

```python
import jax
import jax.numpy as jnp
from jax import lax
from jax.experimental import pallas as pl
from jax.experimental.pallas import tpu as pltpu
from jax.sharding import PartitionSpec as P

outer_rate = 0.7
momentum_decay = 0.9
mix_weight = 0.5

f32, bf16 = jnp.float32, jnp.bfloat16
NX, NZ, NC = 4, 2, 2
CUT = 256
HOLD = 14
WHOLE = pl.BlockSpec(memory_space=pltpu.VMEM)
FAR = pl.BlockSpec(memory_space=pltpu.HBM)
INDEX = pl.BlockSpec(memory_space=pltpu.SMEM)
DMAS = pltpu.SemaphoreType.DMA


def fsdp_perm(dz, dx, dc):
    pairs = []
    for z in range(NZ):
        for x in range(NX):
            for c in range(NC):
                there = (((z + dz) % NZ) * NX + (x + dx) % NX) * NC + (c + dc) % NC
                pairs.append(((z * NX + x) * NC + c, there))
    return pairs


PLUS, MINUS = fsdp_perm(0, 1, 0), fsdp_perm(0, -1, 0)
ACROSS, OTHER_CORE, DIAGONAL = fsdp_perm(1, 0, 0), fsdp_perm(0, 0, 1), fsdp_perm(1, 0, 1)


def send(array, pairs):
    return lax.ppermute(array, "fsdp", pairs)


def after(value, *earlier):
    return lax.optimization_barrier((value, *earlier))[0]


def call(kernel, name, in_specs, out_specs, out_shape, operands, scratch=(), aliases={}, limit=16, traffic=2):
    return pl.pallas_call(
        kernel,
        in_specs=in_specs,
        out_specs=out_specs,
        out_shape=out_shape,
        scratch_shapes=scratch,
        input_output_aliases=aliases,
        compiler_params=pltpu.CompilerParams(vmem_limit_bytes=limit * 1024 * 1024),
        cost_estimate=pl.CostEstimate(flops=0, bytes_accessed=traffic * 1024 * 1024, transcendentals=0),
        name=name,
    )(*operands)


def dot(a, b, ca, cb):
    return lax.dot_general(a, b, (((ca,), (cb,)), ((), ())), preferred_element_type=f32)


def columns(whole, place, width):
    return whole.at[:, pl.ds(pl.multiple_of(place * width, width), width)]


FIRST, SECOND = (6, 2), (4, 5, 7, 0, 1, 3)


def select_kernel(places, tokens, cot, first, second, sems):
    width = cot.shape[1]
    copies = [pltpu.make_async_copy(cot, first.at[len(FIRST)], sems.at[8])]
    for out, blocks in ((first, FIRST), (second, SECOND)):
        for i, b in enumerate(blocks):
            copies.append(pltpu.make_async_copy(columns(tokens, places[b], width), out.at[i], sems.at[b]))
    for copy in copies:
        copy.start()
    for copy in copies:
        copy.wait()


def select(places, tokens, cot):
    return call(
        select_kernel,
        "select",
        [INDEX, WHOLE, WHOLE],
        [WHOLE] * 2,
        [jax.ShapeDtypeStruct((count, *cot.shape), bf16) for count in (len(FIRST) + 1, len(SECOND))],
        (places, tokens, cot),
        [DMAS((9,))],
        traffic=4,
    )


def block_of(tokens, place, width):
    return tokens[:, pl.ds(pl.multiple_of(place * width, width), width)]


def partner_block(par, b):
    first, second = par
    return first[FIRST.index(b)] if b in FIRST else second[SECOND.index(b)]


def partial(b, places, tokens, cot, *par):
    own = block_of(tokens, places[b], cot.shape[1])
    return dot(own, cot[...], 0, 0) + dot(partner_block(par, b), par[0][len(FIRST)], 0, 0)


ROWS = [INDEX] + [WHOLE] * 4


def far_kernel(*refs):
    *rows, top, bottom = refs
    half = top.shape[1]
    for i, b in enumerate((6, 2)):
        block = partial(b, *rows)
        top[i] = block[:half].astype(bf16)
        bottom[i] = block[half:].astype(bf16)


def far_partials(*rows):
    width = rows[2].shape[1]
    return call(
        far_kernel,
        "far_partials",
        ROWS,
        [WHOLE] * 2,
        [jax.ShapeDtypeStruct((2, width // 2, width), bf16)] * 2,
        rows,
        traffic=5,
    )


def relay_kernel(part, *refs):
    rows, (top, bottom), outs = refs[:5], refs[5:7], refs[7:]
    plus, minus = outs[: len(outs) // 2], outs[len(outs) // 2 :]
    half = top.shape[1]
    for k, pieces, arrived, at in ((1, plus, top, 0), (3, minus, bottom, half)):
        block = partial(4 - 4 * part + k, *rows)
        row = 0
        for piece in pieces:
            count = piece.shape[0]
            low, high = max(row, at), min(row + count, at + half)
            if row < low:
                piece[: min(low - row, count)] = block[row : min(low, row + count)].astype(bf16)
            if low < high:
                mine = arrived[part, low - at : high - at].astype(f32)
                piece[low - row : high - row] = (block[low:high] + mine).astype(bf16)
            if max(high, row) < row + count and low < row + count:
                start = max(high, row)
                piece[start - row :] = block[start : row + count].astype(bf16)
            row += count


def relay(rows, top, bottom, part, cuts):
    width = rows[2].shape[1]
    return call(
        lambda *refs: relay_kernel(part, *refs),
        "relay",
        ROWS + [WHOLE] * 2,
        [WHOLE] * (2 * len(cuts)),
        [jax.ShapeDtypeStruct((count, width), bf16) for count in cuts] * 2,
        (*rows, top, bottom),
        traffic=5,
    )


def closing_kernel(part, *refs):
    *rows, left, right, out = refs
    total = partial(4 - 4 * part, *rows)
    count = left.shape[0]
    added = total[:count] + left[...].astype(f32) + right[...].astype(f32)
    out[:count] = added.astype(out.dtype)
    if count < out.shape[0]:
        out[count:] = total[count:].astype(out.dtype)


def closing(rows, left, right, part):
    width = rows[2].shape[1]
    return call(
        lambda *refs: closing_kernel(part, *refs),
        "closing",
        ROWS + [WHOLE] * 2,
        WHOLE,
        jax.ShapeDtypeStruct((width, width), f32 if part else bf16),
        (*rows, left, right),
        traffic=4,
    )


def finish_kernel(total, across, left, right, out):
    out[:CUT] = total[:CUT] + across[:CUT].astype(f32)
    late = left[...].astype(f32) + right[...].astype(f32)
    out[CUT:] = total[CUT:] + across[CUT:].astype(f32) + late


def finish(total, across, left, right):
    return call(
        finish_kernel,
        "finish",
        [WHOLE] * 4,
        WHOLE,
        jax.ShapeDtypeStruct(total.shape, f32),
        (total, across, left, right),
    )


def apply_kernel(part, *refs):
    rows, (w0, w1, w2a, w2b, w3), rest = refs[:5], refs[5:10], refs[10:]
    places, tokens, cot, *par = rows
    if part:
        v_own_in, v_par_in, _, v_own, grad, *back, ready, sems = rest
    else:
        v_own, v_par, grad, *back, ready, sems = rest
    par_cot = par[0].at[len(FIRST)]
    width = cot.shape[1]
    half = w2a.shape[0]
    copies = []
    sums = [v_own_in[...], v_par_in[...]] if part else [0.0, 0.0]
    for k, w in enumerate((w0, w1, None, w3)):
        pieces = [(w, slice(0, width))] if k != 2 else [(w2a, slice(0, half)), (w2b, slice(half, width))]
        b = 4 * part + k
        blocks = (block_of(tokens, places[b], width), partner_block(par, b))
        for n, block in enumerate(blocks):
            sums[n] += sum(dot(block[:, s], p[...], 1, 0) for p, s in pieces)
        for p, s in pieces:
            ready[k, :, s] = dot(cot[...], p[...], 1, 1).astype(bf16)
            returned = dot(par_cot[...], p[...], 1, 1).astype(bf16)
            if part:
                back[k][: returned.shape[0], s] = returned
            else:
                back[k // 2][k % 2, :, s] = returned
        copy = pltpu.make_async_copy(ready.at[k], columns(grad, places[b], width), sems.at[k])
        copy.start()
        copies.append(copy)
    v_own[...] = sums[0]
    if part:
        rows_each = cot.shape[0] // 4
        for k in range(4):
            back[k][cot.shape[0] :] = sums[1][k * rows_each : (k + 1) * rows_each].astype(bf16)
    else:
        v_par[...] = sums[1]
    for copy in copies:
        copy.wait()


def apply_weight(rows, pieces, carry, part):
    tokens, cot = rows[1:3]
    operands = (*rows, *pieces, *carry)
    total = jax.ShapeDtypeStruct(cot.shape, f32)
    whole = jax.ShapeDtypeStruct(tokens.shape, bf16)
    count, width = cot.shape
    shapes = [(count + count // 4, width)] * 4 if part else [(2, count, width)] * 2
    back = [jax.ShapeDtypeStruct(shape, bf16) for shape in shapes]
    return call(
        lambda *refs: apply_kernel(part, *refs),
        "apply_weight",
        ROWS + [WHOLE] * 5 + ([WHOLE, WHOLE, FAR] if part else []),
        [WHOLE] * (2 - part) + [FAR] + [WHOLE] * len(back),
        [total] * (2 - part) + [whole] + back,
        operands,
        [pltpu.VMEM((4, *cot.shape), bf16), DMAS((4,))],
        {len(operands) - 1: 1} if part else {},
        traffic=4,
    )


def place_kernel(part, places, *rest):
    if part:
        *blocks, v_own, _, out, values, sems = rest
        count = v_own.shape[0]
        sources = [block.at[pl.ds(0, count)] for block in blocks]
    else:
        *blocks, _, out, sems = rest
        sources = [block.at[k] for block in blocks for k in range(2)]
    width = sources[0].shape[-1]
    copies = [
        pltpu.make_async_copy(source, columns(out, places[4 * part + k], width), sems.at[k])
        for k, source in enumerate(sources)
    ]
    for copy in copies:
        copy.start()
    if part:
        for k, block in enumerate(blocks):
            at = slice(k * count // 4, (k + 1) * count // 4)
            values[at] = (v_own[at] + block[count:].astype(f32)).astype(bf16)
    for copy in copies:
        copy.wait()


def place(places, blocks, whole, v_own, part):
    operands = (places, *blocks, v_own, whole) if part else (places, *blocks, whole)
    out = jax.ShapeDtypeStruct(whole.shape, bf16)
    return call(
        lambda *refs: place_kernel(part, *refs),
        "place",
        [INDEX] + [WHOLE] * (len(operands) - 2) + [FAR],
        [FAR, WHOLE] if part else FAR,
        [out, jax.ShapeDtypeStruct(v_own.shape, bf16)] if part else out,
        operands,
        [DMAS((4,))],
        {len(operands) - 1: 0},
        traffic=5,
    )


def partner(part, bits):
    return lax.ppermute(part, "replica", [(i, i ^ bits) for i in range(16)])


def outer_kernel(fragment, delta, moment, whole, local, new_global, new_moment, new_local):
    averaged = delta[...] / 16.0
    moment_next = momentum_decay * moment[0] + averaged
    global_next = whole[0] - outer_rate * (averaged + momentum_decay * moment_next)
    new_moment[...] = moment_next
    new_global[...] = global_next
    new_local[0] = mix_weight * local[0, 0] + (1.0 - mix_weight) * global_next


def outer_step(fragment, delta, moment, whole, local):
    rows, width = delta.shape
    flat = pl.BlockSpec((rows, width), lambda i, f: (0, 0))
    chosen = pl.BlockSpec((1, rows, width), lambda i, f: (f[0], 0, 0))
    return pl.pallas_call(
        outer_kernel,
        grid_spec=pltpu.PrefetchScalarGridSpec(
            num_scalar_prefetch=1,
            grid=(1,),
            in_specs=[flat, chosen, chosen, pl.BlockSpec((1, 1, rows, width), lambda i, f: (0, f[0], 0, 0))],
            out_specs=[flat, flat, pl.BlockSpec((1, rows, width), lambda i, f: (0, 0, 0))],
        ),
        out_shape=[jax.ShapeDtypeStruct((rows, width), f32)] * 2 + [jax.ShapeDtypeStruct((1, rows, width), f32)],
        compiler_params=pltpu.CompilerParams(vmem_limit_bytes=8 * 1024 * 1024),
        cost_estimate=pl.CostEstimate(flops=0, bytes_accessed=1024 * 1024, transcendentals=0),
        name="outer_step",
    )(fragment, delta, moment, whole, local)


def hold_kernel(places, _, out):
    for b in range(8):
        out[b] = places[b]


def hold(places, array, traffic):
    return call(
        hold_kernel,
        "hold",
        [INDEX, FAR],
        INDEX,
        jax.ShapeDtypeStruct(places.shape, places.dtype),
        (places, array),
        traffic=traffic,
    )


def body(
    tokens, cotangent, w_value, outer_global, outer_momentum, local_params, outer_delta, fragment
):
    me = lax.axis_index("fsdp")
    core, x, z = lax.rem(me, NC), lax.rem(me // NC, NX), me // (NC * NX)
    steps = jnp.arange(8, dtype=jnp.int32)
    chips = lax.rem(z + steps // NX, NZ) * NX + lax.rem(x + steps, NX)
    own = chips * NC + core
    other = chips * NC + (1 - core)

    shard = w_value[0]
    width = shard.shape[1]
    half = shard.shape[0] // 2
    par = [send(piece, OTHER_CORE) for piece in select(other, tokens, cotangent)]
    behind, ahead = send(shard, PLUS), send(shard, MINUS)
    shard_across = send(shard, ACROSS)

    rows = (own, tokens, cotangent, *par)
    top, bottom = far_partials(*rows)
    delta = outer_delta[0] + partner(outer_delta[0], 1)
    gate = top
    top, bottom = send(top, PLUS), send(bottom, MINUS)
    far_top = send(after(behind[:half], gate), PLUS)
    far_bottom = send(after(ahead[half:], gate), MINUS)

    across_in = hold(own, after(shard_across, delta), HOLD)
    top, bottom, far_top, far_bottom = lax.optimization_barrier((top, bottom, far_top, far_bottom))
    plus, minus = relay((across_in, *rows[1:]), top, bottom, 0, (width,))
    from_left, from_right = send(plus, PLUS), send(minus, MINUS)
    delta = after(delta, plus)
    delta = sum((partner(delta, bits) for bits in (4, 8, 12)), delta)
    pieces = (shard, ahead, after(far_top, delta), far_bottom, behind)
    v_own, v_par, grad, *back = apply_weight(rows, pieces, (), 0)
    back = [send(piece, OTHER_CORE) for piece in back]

    shard_across = after(shard_across, from_left, from_right, v_own, across_in)
    behind, ahead = send(shard_across, PLUS), send(shard_across, MINUS)
    across = closing((across_in, *rows[1:]), from_left, from_right, 0)
    from_across = send(across, ACROSS)
    delta = delta + partner(after(delta, v_own), 2)
    plus, plus_late, minus, minus_late = relay(rows, after(top, across), bottom, 1, (CUT, width - CUT))
    grad = place(other, back, grad, None, 0)

    far_top, far_bottom = send(behind[:half], PLUS), send(ahead[half:], MINUS)
    left, right = send(after(plus, behind), PLUS), send(after(minus, ahead, grad), MINUS)
    pieces = (shard_across, ahead, far_top, far_bottom, behind)
    v_own, grad, *back = apply_weight(rows, pieces, (v_own, v_par, grad), 1)
    everything = (v_own, from_across, delta, left, right)
    left_late = send(after(plus_late, *everything), PLUS)
    right_late = send(after(minus_late, *everything), MINUS)
    back = [send(piece, OTHER_CORE) for piece in back]
    total = closing(rows, left, right, 1)
    grad, values = place(after(other, total), back, grad, v_own, 1)
    grad_weight = finish(after(total, grad, values), from_across, left_late, right_late)

    new_global, new_momentum, new_local = outer_step(
        fragment, delta, outer_momentum, outer_global, local_params
    )
    return (values, grad, grad_weight[None], new_global, new_momentum, new_local)


def solution(mesh):
    in_specs = (
        P(("replica", "fsdp"), None),
        P(("replica", "fsdp"), None),
        P("replica", "fsdp", None),
        P(None, "fsdp", None),
        P(None, "fsdp", None),
        P("replica", None, "fsdp", None),
        P("replica", "fsdp", None),
        P(),
    )
    out_specs = (
        P(("replica", "fsdp"), None),
        P(("replica", "fsdp"), None),
        P("replica", "fsdp", None),
        P("fsdp", None),
        P("fsdp", None),
        P("replica", "fsdp", None),
    )
    return jax.shard_map(body, mesh=mesh, in_specs=in_specs, out_specs=out_specs, check_vma=False)
```
